256 devices in a mesh: dp: 8 (over y, core), expert: 32 (over x, z).
Axes of the slice: x: 4, y: 4, z: 8, core: 2. Of those that a mesh axis runs over, the one named last changes fastest.
Arguments:
- weight: bfloat16 [32, 1024, 7168], P('expert', 'dp'), may hold values from -6 to 6
- first_moment: float32 [32, 1024, 256], P('expert', 'dp'), may hold values from -6 to 6
- second_moment: float32 [32, 1024, 256], P('expert', 'dp'), may hold values from 0.05 to 1
- projector_old: bfloat16 [32, 7168, 256], P('expert', 'dp'), may hold values from -0.0625 to 0.0625
- projector_new: bfloat16 [32, 7168, 256], P('expert', 'dp'), may hold values from -0.0625 to 0.0625
- change_flag: int32 [32], replicated, may hold values 0 or 1
- partner: int32 [32], replicated, may hold values from 0 to 31, as said below
- hidden_act: bfloat16 [65536, 1024], P(('dp', 'expert')), may hold values from -6 to 6
- out_grad: bfloat16 [65536, 7168], P(('dp', 'expert')), may hold values from -0.125 to 0.125
- route: int32 [65536, 1], P(('dp', 'expert')), may hold values from 0 to 31; in each aligned block of 256 rows (0 to 255, 256 to 511, ...) at most 16 rows name the same one
Outputs:
- new_weight: bfloat16 [32, 1024, 7168], P('expert', 'dp')
- new_first: float32 [32, 1024, 256], P('expert', 'dp')
- new_second: float32 [32, 1024, 256], P('expert', 'dp')
- new_projector: bfloat16 [32, 7168, 256], P('expert', 'dp')
The draws below stay inside these ranges and needn't reach their ends.
Inputs may be any that keep to these rules, and one draw needn't show every extreme that they name: partner[i] = i XOR c for one c of 1 to 31 in each draw; so partner[partner[i]] = i. `route`: the 256 rows of one device name any one expert at most 16 times, a bound that some block reaches.
All inputs are finite; a program needn't handle non-finite values.
Results may differ from the reference program's by a relative error of at most 0.014.
Values may be sent and summed in bfloat16 or wider, within the bound.
A program may use at most 128 MiB of HBM per device.

```python
import math
import jax
import jax.numpy as jnp
import numpy as np
from jax import lax

D = 7168
FF = 1024
RANK = 256
TOK_DEV = 256
EXPERTS = 32
CAP = 16
TOKENS = 65536
N_DP = 8
N_EXPERT = 32


def draw_partner(key, part):
    shift_mask = jax.random.randint(key, (), 1, EXPERTS, dtype=jnp.int32)
    return jnp.bitwise_xor(jnp.arange(EXPERTS, dtype=jnp.int32), shift_mask)


def plant(result, own_key, smallest, high):
    shape = result.shape
    place = [jax.random.randint(jax.random.fold_in(own_key, axis), (), 0, shape[axis]) for axis in range(len(shape))]
    result = result.at[tuple(place)].set(smallest)
    longest = shape.index(max(shape))
    place[longest] = (place[longest] + 1) % shape[longest]
    return result.at[tuple(place)].set(high)


def level_of(rng, shape, cuts, low, largest):
    level = 1.0
    for dim, shards_of in cuts:
        draws = jax.random.uniform(jax.random.fold_in(jax.random.fold_in(rng, 6), dim), (shards_of,), jnp.float32, low / len(cuts), largest / len(cuts))
        level = level * jnp.repeat(jnp.exp(draws), shape[dim] // shards_of).reshape((-1,) + (1,) * (len(shape) - 1 - dim))
    return level


def deal_out(stream_key, own, number, rows, count, top, most, slope):
    order = jax.random.permutation(stream_key, count)
    packed, common = load_shares(count, rows * top, most, slope, True), load_shares(count, rows * top, most, slope, False)
    places = jnp.arange(count)

    def named(lengths, turn):
        used = int((lengths > 0).sum())
        fixed = max(1, used // 4)
        shifted = fixed + (places - fixed + turn * (used - fixed)) % max(1, count - fixed)
        return jnp.zeros((count,), jnp.int32).at[order[jnp.where(places < fixed, places, shifted)]].set(jnp.asarray(lengths, jnp.int32))

    lengths = jnp.where(number % 4 == 0, named(packed, number // 4), named(common, number - number // 4 - 1))
    mixed = jax.random.permutation(jax.random.fold_in(own, 3), count)
    donor, receiver = mixed[0:count // 2 * 2:2], mixed[1:count // 2 * 2:2]
    room = jnp.minimum(lengths[donor] - 1, most - lengths[receiver]) // 2
    room = jnp.where((donor == order[0]) | (receiver == order[0]) | (lengths[receiver] == 0), 0, jnp.maximum(room, 0))
    shifted = jax.random.randint(jax.random.fold_in(own, 4), (count // 2,), 0, 1 << 20) % (room + 1)
    lengths = lengths.at[donor].add(-shifted).at[receiver].add(shifted)
    items = jnp.searchsorted(jnp.cumsum(lengths), jnp.arange(rows * top), side="right").astype(jnp.int32)
    grid = items.reshape(top, rows).T
    grid = grid[jax.random.permutation(jax.random.fold_in(own, 1), rows)]
    turn = jax.random.randint(jax.random.fold_in(own, 2), (rows, 1), 0, top)
    return jnp.take_along_axis(grid, (jnp.arange(top)[None, :] + turn) % top, axis=1)


def load_shares(number_of, total, most, lean, full):
    portions = [(1 << 20) // math.isqrt(standing ** lean) + 1 for standing in range(1, number_of + 1)]
    largest = most if full else min(most, max(-(-total // number_of), total * portions[0] // sum(portions)))
    least = 1 if total - largest >= number_of - 1 else 0
    counts, surplus = [largest] + [least] * (number_of - 1), total - largest - least * (number_of - 1)
    while surplus > 0:
        movable = [i for i in range(1, number_of) if counts[i] < largest] or [i for i in range(1, number_of) if counts[i] < most]
        whole, budget = sum([portions[i] for i in movable]), surplus
        for i in movable:
            extra = min(most - counts[i], max(1, budget * portions[i] // whole), surplus)
            counts[i] = counts[i] + extra
            surplus = surplus - extra
    return np.array(counts)


def scatter_about(rng, shape, deviation, most, pieces=(), kind=jnp.bfloat16):
    gain = level_of(rng, shape, pieces, -0.22, 0.18) if pieces else 1.0
    result = jax.random.normal(rng, shape, jnp.float32) * deviation * gain
    return jnp.minimum(jnp.maximum(result, -most), most).astype(kind)


def setup_inputs(seed: int = 0) -> dict:
    key_list = jax.random.split(jax.random.key(seed), 11)
    weight = scatter_about(key_list[0], (EXPERTS, FF, D), 1.0, 6.0, ((0, 32), (1, 8)))
    first_moment = scatter_about(key_list[1], (EXPERTS, FF, RANK), 1.0, 6.0, ((0, 32), (1, 8)), jnp.float32)
    second_moment = jnp.clip(jnp.exp(math.log(1.0) - 2.9957323 * jax.random.uniform(key_list[2], (EXPERTS, FF, RANK), jnp.float32) ** level_of(key_list[2], (EXPERTS, FF, RANK), ((0, 32), (1, 8)), -0.2, 0.2)), 0.05, 1.0)
    projector_old = scatter_about(key_list[3], (EXPERTS, D, RANK), D ** -0.5, 0.0625, ((0, 32), (1, 8)))
    projector_new = scatter_about(key_list[4], (EXPERTS, D, RANK), D ** -0.5, 0.0625, ((0, 32), (1, 8)))
    change_flag = plant((jax.random.randint(key_list[5], (EXPERTS,), 0, 2) < 1).astype(jnp.int32), jax.random.fold_in(key_list[5], 1), 0, 1)
    partner = draw_partner(jax.random.fold_in(key_list[10], 71), 0)
    hidden_act = scatter_about(key_list[7], (TOKENS, FF), 1.0, 6.0, ((0, 256),))
    out_grad = scatter_about(key_list[8], (TOKENS, D), 0.02, 0.125, ((0, 256),))
    route_keys = jax.random.split(jax.random.fold_in(key_list[9], 1), TOKENS // TOK_DEV)
    route_turns = jax.random.permutation(jax.random.fold_in(key_list[9], 3), TOKENS // TOK_DEV)
    route = jax.vmap(lambda own, number: deal_out(jax.random.fold_in(key_list[9], 2), own, number, TOK_DEV, EXPERTS, 1, CAP, 2))(route_keys, route_turns).reshape((TOKENS, 1))
    return dict(weight=weight, first_moment=first_moment, second_moment=second_moment, projector_old=projector_old, projector_new=projector_new, change_flag=change_flag, partner=partner, hidden_act=hidden_act, out_grad=out_grad, route=route)


beta_one = 0.9
beta_two = 0.95
adam_eps = 1e-08
step_size = 2.0

def reference(weight, first_moment, second_moment, projector_old, projector_new, change_flag, partner, hidden_act, out_grad, route):
    token_expert = route[:, 0]
    hidden_pad = jnp.concatenate([hidden_act, jnp.zeros((1, hidden_act.shape[1]), hidden_act.dtype)], axis=0)
    grad_pad = jnp.concatenate([out_grad, jnp.zeros((1, out_grad.shape[1]), out_grad.dtype)], axis=0)
    limit = N_DP * N_EXPERT * CAP

    def one_expert(index):
        old_proj = projector_old[index]
        new_proj = projector_new[index]
        intersection = lax.dot_general(old_proj, new_proj, (((0,), (0,)), ((), ())), preferred_element_type=jnp.float32)
        changed = change_flag[index] > 0
        first_start = jnp.where(changed, jnp.dot(first_moment[index], intersection, precision=lax.Precision.HIGHEST), first_moment[index])
        second_start = jnp.where(changed, jnp.dot(second_moment[index], intersection * intersection, precision=lax.Precision.HIGHEST), second_moment[index])
        active = jnp.where(changed, new_proj, old_proj)
        picked = jnp.nonzero(token_expert == index, size=limit, fill_value=TOKENS)[0].astype(jnp.int32)
        hidden_rows = jnp.take(hidden_pad, picked, axis=0)
        grad_rows = jnp.take(grad_pad, picked, axis=0)
        along = jnp.dot(grad_rows, active, preferred_element_type=jnp.float32)
        proj_grad = jnp.dot(hidden_rows.astype(jnp.float32).T, along, precision=lax.Precision.HIGHEST)
        first_next = beta_one * first_start + (1.0 - beta_one) * proj_grad
        second_next = beta_two * second_start + (1.0 - beta_two) * proj_grad * proj_grad
        direction = (first_next / (jnp.sqrt(second_next) + adam_eps)).astype(jnp.bfloat16)
        update = lax.dot_general(direction, active, (((1,), (1,)), ((), ())), preferred_element_type=jnp.float32)
        weight_next = (weight[index].astype(jnp.float32) - step_size * update).astype(jnp.bfloat16)
        return (weight_next, first_next, second_next, active)
    results = lax.map(one_expert, jnp.arange(EXPERTS, dtype=jnp.int32))
    order = partner.astype(jnp.int32)
    return (results[0][order], results[1][order], results[2][order], results[3][order])
```

```python
import jax
import jax.numpy as jnp
from jax import lax
from jax.sharding import PartitionSpec as P

beta_one = 0.9
beta_two = 0.95
adam_eps = 1e-08
step_size = 2.0


def moved(values, shift_mask):
    experts = lax.axis_size("expert")

    def by(mask):
        pairs = [(source, source ^ mask) for source in range(experts)]
        return lambda arrays: tuple(lax.ppermute(array, "expert", pairs) for array in arrays)

    return lax.switch(shift_mask - 1, [by(mask) for mask in range(1, experts)], values)


def per_device(
    weight,
    first_moment,
    second_moment,
    projector_old,
    projector_new,
    change_flag,
    partner,
    hidden_act,
    out_grad,
    route,
):
    experts = lax.axis_size("expert")
    own_index = lax.axis_index("expert")
    shift_mask = partner[0]
    changed = change_flag[own_index] > 0
    old_proj, new_proj = projector_old[0], projector_new[0]
    active_home = jnp.where(changed, new_proj, old_proj)
    intersection = lax.psum(
        lax.dot_general(
            old_proj, new_proj, (((0,), (0,)), ((), ())), preferred_element_type=jnp.float32
        ),
        "dp",
    )
    first_turned = jnp.dot(first_moment[0], intersection, precision=lax.Precision.HIGHEST)
    second_turned = jnp.dot(
        second_moment[0], intersection * intersection, precision=lax.Precision.HIGHEST
    )
    first_start = jnp.where(changed, first_turned, first_moment[0]).astype(jnp.bfloat16)
    second_start = jnp.where(changed, second_turned, second_moment[0]).astype(jnp.bfloat16)

    token_count = hidden_act.shape[0]
    capacity = max(2, 2 * token_count // experts)
    target = jnp.bitwise_xor(route[:, 0], shift_mask)
    columns = jnp.arange(experts, dtype=jnp.int32)
    one_hot = (target[:, None] == columns[None, :]).astype(jnp.int32)
    earlier = jnp.cumsum(one_hot, axis=0) - one_hot
    position = target * capacity + jnp.sum(earlier * one_hot, axis=1)
    slots = jnp.arange(experts * capacity, dtype=jnp.int32)
    pick = (slots[:, None] == position[None, :]).astype(jnp.bfloat16)
    send_hidden = jnp.dot(pick, hidden_act, preferred_element_type=jnp.bfloat16)
    send_grad = jnp.dot(pick, out_grad, preferred_element_type=jnp.bfloat16)
    weight_here, active, first_start, second_start = moved(
        (weight[0], active_home, first_start, second_start), shift_mask
    )
    got_hidden = lax.all_to_all(send_hidden, "expert", split_axis=0, concat_axis=0, tiled=True)
    got_grad = lax.all_to_all(send_grad, "expert", split_axis=0, concat_axis=0, tiled=True)
    projector_full = lax.all_gather(active, "dp", axis=0, tiled=True)
    along = jnp.dot(got_grad, projector_full, preferred_element_type=jnp.float32)
    partial_grad = lax.dot_general(
        got_hidden.astype(jnp.float32),
        along,
        (((0,), (0,)), ((), ())),
        precision=lax.Precision.HIGHEST,
    )
    proj_grad = lax.psum_scatter(
        partial_grad.astype(jnp.bfloat16), "dp", scatter_dimension=0, tiled=True
    ).astype(jnp.float32)
    first_next = beta_one * first_start.astype(jnp.float32) + (1.0 - beta_one) * proj_grad
    second_next = (
        beta_two * second_start.astype(jnp.float32) + (1.0 - beta_two) * proj_grad * proj_grad
    )
    direction = (first_next / (jnp.sqrt(second_next) + adam_eps)).astype(jnp.bfloat16)
    update = lax.dot_general(
        direction, projector_full, (((1,), (1,)), ((), ())), preferred_element_type=jnp.float32
    )
    new_weight = (weight_here.astype(jnp.float32) - step_size * update).astype(jnp.bfloat16)
    return (new_weight[None], first_next[None], second_next[None], active[None])


def solution(mesh):
    in_specs = (
        P("expert", "dp", None),
        P("expert", "dp", None),
        P("expert", "dp", None),
        P("expert", "dp", None),
        P("expert", "dp", None),
        P(),
        P(),
        P(("dp", "expert"), None),
        P(("dp", "expert"), None),
        P(("dp", "expert"), None),
    )
    out_specs = (
        P("expert", "dp", None),
        P("expert", "dp", None),
        P("expert", "dp", None),
        P("expert", "dp", None),
    )
    return jax.shard_map(
        per_device, mesh=mesh, in_specs=in_specs, out_specs=out_specs, check_vma=False
    )
```

```python
import jax
import jax.numpy as jnp
from jax import lax
from jax.experimental import pallas as pl
from jax.experimental.pallas import tpu as pltpu
from jax.sharding import PartitionSpec as P

beta_one = 0.9
beta_two = 0.95
adam_eps = 1e-08
step_size = 2.0

NX, NY, NZ = 4, 4, 8
EX = NX * NZ
CAP = 16
SLOTS = EX * CAP
PEERS = NX * NY
HALF = NZ // 2
MESH = pl.DeviceIdType.MESH
CONTRACT_ROWS = (((0,), (0,)), ((), ()))


def one_hot(pos_row, first=0, count=SLOTS):
    slot = first + lax.broadcasted_iota(jnp.int32, (count, pos_row.shape[1]), 0)
    return jnp.where(slot == pos_row, 1.0, 0.0).astype(jnp.bfloat16)


def exchange_kernel(
    c_ref,
    grad,
    hidden,
    act4,
    pos_home,
    pos_target,
    pg_out,
    full_out,
    tok,
    pos_all,
    proj,
    srt,
    alg,
    y_send,
    y_recv,
    h_send,
    h_recv,
    a_send,
    a_recv,
    p_send,
    p_recv,
    sel,
    total,
    loc_sem,
    xs_sem,
    xr_sem,
    ts_sem,
    tr_sem,
    ps_sem,
    pr_sem,
    rs_sem,
    rr_sem,
    ls_sem,
    lr_sem,
    ss_sem,
    sr_sem,
    ys_sem,
    yr_sem,
    hs_sem,
    hr_sem,
    as_sem,
    ar_sem,
    gs_sem,
    gr_sem,
    ns_sem,
    nr_sem,
    fs_sem,
    fr_sem,
    us_sem,
    ur_sem,
):
    d = lax.axis_index("dp")
    e = lax.axis_index("expert")
    x, z = e // NZ, e % NZ
    y, core = d // 2, d % 2
    me = x * NY + y
    tokens = hidden.shape[0]
    rows = full_out.shape[0] // (2 * NY)
    sibling = (2 * y + 1 - core, e)

    def plane(k):
        px, py = (x + k % NX) % NX, (y + k // NX) % NY
        return px, py, (2 * py + core, px * NZ + z)

    def plane_from(k):
        px, py = (x + NX - k % NX) % NX, (y + NY - k // NX) % NY
        return px * NY + py

    def remote(src, dst, send, recv, device):
        return pltpu.make_async_remote_copy(
            src, dst, send, recv, device_id=device, device_id_type=MESH
        )

    def repeat(low, high, do):
        def step(k, carry):
            do(k)
            return carry

        lax.fori_loop(low, high, step, 0)

    def settle(view, sem):
        pltpu.make_async_copy(view, view, sem).wait()

    drain = []
    barrier = pltpu.get_barrier_semaphore()

    def greet(device):
        pl.semaphore_signal(barrier, inc=1, device_id=device, device_id_type=MESH)

    repeat(1, EX, lambda k: greet((d, (e + k) % EX)))
    repeat(NX, PEERS, lambda k: greet(plane(k)[2]))
    repeat(0, NY, lambda k: greet((2 * ((y + k) % NY) + 1 - core, e)))
    pl.semaphore_wait(barrier, EX - 1 + PEERS - NX + NY)

    mine = pl.ds(pl.multiple_of(core * 256, 256), 256)

    def proj_copy(k):
        px = (x + k) % NX
        return remote(
            act4.at[px], proj.at[x, z, mine], xs_sem, xr_sem, (d, px * NZ + z)
        )

    def columns(px, py, part):
        start = (2 * py + part) * rows + (2 * px - px // 3) * 128
        return pl.ds(pl.multiple_of(start, 128), 256)

    def tok_copy(k, part):
        px, py, device = plane(k)
        return remote(
            grad.at[:, columns(px, py, part)],
            tok.at[me, :, pl.ds(part * 256, 256)],
            ts_sem,
            tr_sem.at[me],
            device,
        )

    def pos_copy(k):
        return remote(pos_home, pos_all.at[me], ps_sem, pr_sem.at[me], plane(k)[2])

    for k in range(1, NX):
        proj_copy(k).start()
    drain.append((act4.at[pl.ds(0, NX - 1)], xs_sem))
    own_proj = pltpu.make_async_copy(act4.at[x], proj.at[x, z, mine], loc_sem.at[0])
    own_proj.start()
    repeat(1, PEERS, lambda k: pos_copy(k).start())
    drain.append((pos_all.at[pl.ds(0, PEERS - 1)], ps_sem))

    def start_tok(k):
        tok_copy(k, 0).start()
        tok_copy(k, 1).start()

    repeat(1, PEERS, start_tok)
    drain.append((tok.at[pl.ds(0, PEERS - 1)], ts_sem))
    own_tok = [
        pltpu.make_async_copy(
            grad.at[:, columns(x, y, part)],
            tok.at[me, :, pl.ds(part * 256, 256)],
            loc_sem.at[1 + part],
        )
        for part in range(2)
    ]
    for copy in own_tok:
        copy.start()
    pos_all[me] = pos_home[...]

    def sort_hidden(i):
        chunk = pl.ds(pl.multiple_of(i * 64, 64), 64)
        h_send[chunk] = jnp.dot(
            one_hot(pos_target[0:1], i * 64, 64),
            hidden[...],
            preferred_element_type=jnp.float32,
        ).astype(jnp.bfloat16)

    repeat(0, SLOTS // 64, sort_hidden)

    own_proj.wait()
    settle(proj.at[pl.ds(0, NX - 1), 0, pl.ds(0, 256)], xr_sem)

    def ring_copy(step, right):
        if right:
            zz, to, send, recv = (z + NZ - step + 1) % NZ, (z + 1) % NZ, rs_sem, rr_sem
        else:
            zz, to, send, recv = (z + step - 1) % NZ, (z + NZ - 1) % NZ, ls_sem, lr_sem
        xs = pl.ds(0, NX)
        if step == HALF:
            xs = pl.ds(0 if right else NX // 2, NX // 2)
        view = proj.at[xs, zz, mine]
        return remote(view, view, send.at[step - 1], recv.at[step - 1], (d, x * NZ + to))

    def sib_copy(zz):
        view = proj.at[:, zz, mine]
        return remote(view, view, ss_sem.at[zz], sr_sem.at[zz], sibling)

    def ring_drain():
        for step in range(1, HALF + 1):
            ring_copy(step, True).wait_send()
            ring_copy(step, False).wait_send()
        repeat(0, NZ, lambda k: sib_copy(k).wait_send())

    def sort_block(k):
        slot = plane_from(k)
        settle(tok.at[slot], tr_sem.at[slot])
        settle(pos_all.at[slot], pr_sem.at[slot])
        sort_slot(slot)

    def sort_slot(slot):
        rows_of = pl.ds(pl.multiple_of(slot * CAP, CAP), CAP)

        def sort_part(i):
            sorted_rows = jnp.dot(
                one_hot(pos_all[slot, 0:1], i * 8 * CAP, 8 * CAP),
                tok[slot],
                preferred_element_type=jnp.float32,
            ).astype(jnp.bfloat16)
            srt[pl.ds(i * 8, 8), rows_of, :] = sorted_rows.reshape(8, CAP, 512)

        repeat(0, EX // 8, sort_part)

    def hid_copy(k):
        to = (e + k) % EX
        return remote(
            h_send.at[pl.ds(pl.multiple_of(to * CAP, CAP), CAP)],
            h_recv.at[pl.ds(pl.multiple_of(e * CAP, CAP), CAP)],
            hs_sem,
            hr_sem,
            (d, to),
        )

    ring_copy(1, True).start()
    ring_copy(1, False).start()
    sib_copy(z).start()
    for copy in own_tok:
        copy.wait()
    sort_slot(me)
    bounds = [1, 3, 6, 9, 11]
    others = pl.ds(0, SLOTS - CAP)
    for step in range(1, HALF + 1):
        repeat(bounds[step - 1], bounds[step], sort_block)
        ring_copy(step, True).wait_recv()
        if step < HALF:
            ring_copy(step + 1, True).start()
        ring_copy(step, False).wait_recv()
        if step < HALF:
            ring_copy(step + 1, False).start()
            sib_copy((z + NZ - step) % NZ).start()
            sib_copy((z + step) % NZ).start()
        else:
            sib_copy((z + HALF) % NZ).start()
        if step == HALF - 1:
            repeat(1, EX, lambda k: hid_copy(k).start())
            drain.append((h_send.at[others], hs_sem))
    repeat(bounds[HALF], PEERS, sort_block)
    repeat(0, NZ, lambda k: sib_copy(k).wait_recv())

    own_rows = pl.ds(pl.multiple_of(e * CAP, CAP), CAP)
    h_recv[own_rows] = h_send[own_rows]

    def multiply(index):
        alg[index] = jnp.dot(
            srt[index], proj[index // NZ, index % NZ], preferred_element_type=jnp.float32
        ).astype(jnp.bfloat16)

    repeat(0, EX, multiply)

    def unsorted(slot):
        block = alg[:, pl.ds(pl.multiple_of(slot * CAP, CAP), CAP), :].reshape(SLOTS, 256)
        return lax.dot_general(
            one_hot(pos_all[slot, 0:1]),
            block,
            CONTRACT_ROWS,
            preferred_element_type=jnp.float32,
        ).astype(jnp.bfloat16)

    def y_copy(k):
        px, py, device = plane(k)
        return remote(y_send.at[px * NY + py], y_recv.at[me], ys_sem, yr_sem, device)

    def send_y(k):
        px, py, _ = plane(k)
        y_send[px * NY + py] = unsorted(px * NY + py)

        @pl.when(k > 0)
        def _():
            y_copy(k).start()

    repeat(0, PEERS, send_y)
    drain.append((y_send.at[pl.ds(0, PEERS - 1)], ys_sem))
    y_recv[me] = y_send[me]

    shift = c_ref[0]
    for px in range(NX):
        from_expert = jnp.bitwise_xor(px * NZ + z, shift)
        sel[px] = proj[from_expert // NZ, from_expert % NZ, mine, :]

    def sel_copy(px, last):
        size = 128 if last else 256
        off = 128 if last else 0
        dst = full_out.at[pl.ds(pl.multiple_of(d * rows + x * 256, 128), size)]
        return sel.at[px, pl.ds(off, size)], dst

    def sel_start(last):
        for k in range(1, NX):
            px = (x + k) % NX
            src, dst = sel_copy(px, last)
            remote(src, dst, ns_sem, nr_sem, (d, px * NZ + z)).start()
        src, dst = sel_copy(x, last)
        own = pltpu.make_async_copy(src, dst, loc_sem.at[3])
        own.start()
        own.wait()

    @pl.when(x < NX - 1)
    def _():
        sel_start(False)

    @pl.when(x == NX - 1)
    def _():
        sel_start(True)

    def sel_settle():
        @pl.when(x < NX - 1)
        def _():
            settle(full_out.at[pl.ds(0, rows - 256)], nr_sem)
            settle(sel.at[pl.ds(0, NX - 1)], ns_sem)

        @pl.when(x == NX - 1)
        def _():
            settle(full_out.at[pl.ds(0, rows - 128)], nr_sem)
            settle(sel.at[pl.ds(0, NX - 1), pl.ds(0, 128)], ns_sem)

    sel_settle()

    def full_rows(which):
        return full_out.at[pl.ds(pl.multiple_of(which * rows, 128), rows)]

    def full_copy(k):
        py = (y + k) % NY
        return remote(
            full_rows(d), full_rows(d), fs_sem, fr_sem.at[k], (2 * py + core, e)
        )

    def up_copy(k):
        view = full_rows(2 * ((y + NY - k) % NY) + core)
        return remote(view, view, us_sem, ur_sem, sibling)

    for k in range(1, NY):
        full_copy(k).start()
    up_copy(0).start()
    drain.append((full_out.at[pl.ds(0, (NY - 1) * rows)], fs_sem))
    drain.append((full_out.at[pl.ds(0, NY * rows)], us_sem))
    drain.append((full_out.at[pl.ds(0, NY * rows)], ur_sem))

    def up_rest():
        for k in range(1, NY):
            full_copy(k).wait_recv()
            up_copy(k).start()

    settle(y_recv.at[pl.ds(0, PEERS - 1)], yr_sem)

    def add_up(i):
        chunk = pl.ds(pl.multiple_of(i * 32, 32), 32)
        total[chunk] = jnp.sum(y_recv[:, chunk, :].astype(jnp.float32), axis=0).astype(
            jnp.bfloat16
        )

    repeat(0, tokens // 32, add_up)

    def sort_total(i):
        chunk = pl.ds(pl.multiple_of(i * 128, 128), 128)
        a_send[chunk] = jnp.dot(
            one_hot(pos_target[0:1], i * 128, 128),
            total[...],
            preferred_element_type=jnp.float32,
        ).astype(jnp.bfloat16)

    repeat(0, SLOTS // 128, sort_total)

    def alg_copy(k):
        to = (e + k) % EX
        return remote(
            a_send.at[pl.ds(pl.multiple_of(to * CAP, CAP), CAP)],
            a_recv.at[pl.ds(pl.multiple_of(e * CAP, CAP), CAP)],
            as_sem,
            ar_sem,
            (d, to),
        )

    repeat(1, EX, lambda k: alg_copy(k).start())
    drain.append((a_send.at[others], as_sem))
    a_recv[own_rows] = a_send[own_rows]
    settle(h_recv.at[others], hr_sem)
    settle(a_recv.at[others], ar_sem)

    ff = p_send.shape[1]

    def outer(part):
        p_send[part] = lax.dot_general(
            h_recv[:, pl.ds(pl.multiple_of(part * ff, ff), ff)],
            a_recv[...],
            CONTRACT_ROWS,
            preferred_element_type=jnp.float32,
        ).astype(jnp.bfloat16)

    repeat(0, 2 * NY, outer)

    def pg_copy(k):
        to = (d + k) % (2 * NY)
        return remote(p_send.at[to], p_recv.at[d], gs_sem, gr_sem, (to, e))

    repeat(1, 2 * NY, lambda k: pg_copy(k).start())
    drain.append((p_send.at[pl.ds(0, 2 * NY - 1)], gs_sem))
    p_recv[d] = p_send[d]
    up_rest()
    settle(p_recv.at[pl.ds(0, 2 * NY - 1)], gr_sem)

    def finish(i):
        chunk = pl.ds(pl.multiple_of(i * 32, 32), 32)
        pg_out[chunk] = jnp.sum(p_recv[:, chunk, :].astype(jnp.float32), axis=0)

    repeat(0, ff // 32, finish)

    ring_drain()
    for view, sem in drain:
        settle(view, sem)


def exchanged(shift_mask, grad, hidden, act4, pos_home, pos_target):
    tokens, width = grad.shape
    ff = hidden.shape[1]
    rows = width // (2 * NY)
    rank = act4.shape[2]
    bf16 = jnp.bfloat16
    vmem = pl.BlockSpec(memory_space=pltpu.VMEM)
    hbm = pl.BlockSpec(memory_space=pl.ANY)
    dma = pltpu.SemaphoreType.DMA
    return pl.pallas_call(
        exchange_kernel,
        out_shape=(
            jax.ShapeDtypeStruct((ff // (2 * NY), rank), jnp.float32),
            jax.ShapeDtypeStruct((width, rank), bf16),
        ),
        in_specs=[pl.BlockSpec(memory_space=pltpu.SMEM), hbm, vmem, vmem, vmem, vmem],
        out_specs=(vmem, hbm),
        scratch_shapes=[
            pltpu.VMEM((PEERS, tokens, 512), bf16),
            pltpu.VMEM((PEERS, 8, tokens), jnp.int32),
            pltpu.VMEM((NX, NZ, 512, rank), bf16),
            pltpu.VMEM((EX, PEERS * CAP, 512), bf16),
            pltpu.VMEM((EX, PEERS * CAP, rank), bf16),
            pltpu.VMEM((PEERS, tokens, rank), bf16),
            pltpu.VMEM((PEERS, tokens, rank), bf16),
            pltpu.VMEM((SLOTS, ff), bf16),
            pltpu.VMEM((SLOTS, ff), bf16),
            pltpu.VMEM((SLOTS, rank), bf16),
            pltpu.VMEM((SLOTS, rank), bf16),
            pltpu.VMEM((2 * NY, ff // (2 * NY), rank), bf16),
            pltpu.VMEM((2 * NY, ff // (2 * NY), rank), bf16),
            pltpu.VMEM((NX, 256, rank), bf16),
            pltpu.VMEM((tokens, rank), bf16),
            dma((4,)),
            dma,
            dma,
            dma,
            dma((PEERS,)),
            dma,
            dma((PEERS,)),
            dma((HALF,)),
            dma((HALF,)),
            dma((HALF,)),
            dma((HALF,)),
            dma((NZ,)),
            dma((NZ,)),
            dma,
            dma,
            dma,
            dma,
            dma,
            dma,
            dma,
            dma,
            dma,
            dma,
            dma,
            dma((NY,)),
            dma,
            dma,
        ],
        compiler_params=pltpu.CompilerParams(
            collective_id=0, has_side_effects=True, vmem_limit_bytes=60 * 1024 * 1024
        ),
        cost_estimate=pl.CostEstimate(
            flops=8_000_000_000, bytes_accessed=400_000_000, transcendentals=0
        ),
        name="project_tokens",
    )(shift_mask, grad, hidden, act4, pos_home, pos_target)


def intersect_kernel(
    old, new, out, parts, landed, summed, rs_sem, rr_sem, gs_sem, gr_sem
):
    d = lax.axis_index("dp")
    e = lax.axis_index("expert")
    group = 2 * NY
    rank = out.shape[0]
    share = rank // group

    def peer(k):
        return (d + k) % group

    def settle(view, sem):
        pltpu.make_async_copy(view, view, sem).wait()

    barrier = pltpu.get_barrier_semaphore()
    for k in range(1, group):
        pl.semaphore_signal(barrier, inc=1, device_id=(peer(k), e), device_id_type=MESH)
    local = lax.dot_general(
        old[...], new[...], CONTRACT_ROWS, preferred_element_type=jnp.float32
    )
    for part in range(group):
        parts[part] = local[part * share : (part + 1) * share]
    pl.semaphore_wait(barrier, group - 1)
    for k in range(1, group):
        pltpu.make_async_remote_copy(
            parts.at[peer(k)],
            landed.at[d],
            rs_sem,
            rr_sem,
            device_id=(peer(k), e),
            device_id_type=MESH,
        ).start()
    landed[d] = parts[d]
    settle(landed.at[pl.ds(0, group - 1)], rr_sem)
    summed[...] = jnp.sum(landed[...], axis=0)
    own = pl.ds(pl.multiple_of(d * share, share), share)
    for k in range(1, group):
        pltpu.make_async_remote_copy(
            summed,
            out.at[own],
            gs_sem,
            gr_sem,
            device_id=(peer(k), e),
            device_id_type=MESH,
        ).start()
    out[own] = summed[...]
    settle(out.at[pl.ds(0, rank - share)], gr_sem)
    settle(landed.at[pl.ds(0, group - 1)], rs_sem)
    settle(landed.at[pl.ds(0, group - 1)], gs_sem)


def intersection_of(old_proj, new_proj):
    rank = old_proj.shape[1]
    share = rank // (2 * NY)
    vmem = pl.BlockSpec(memory_space=pltpu.VMEM)
    return pl.pallas_call(
        intersect_kernel,
        out_shape=jax.ShapeDtypeStruct((rank, rank), jnp.float32),
        in_specs=[vmem, vmem],
        out_specs=vmem,
        scratch_shapes=[
            pltpu.VMEM((2 * NY, share, rank), jnp.float32),
            pltpu.VMEM((2 * NY, share, rank), jnp.float32),
            pltpu.VMEM((share, rank), jnp.float32),
            pltpu.SemaphoreType.DMA,
            pltpu.SemaphoreType.DMA,
            pltpu.SemaphoreType.DMA,
            pltpu.SemaphoreType.DMA,
        ],
        compiler_params=pltpu.CompilerParams(collective_id=1, has_side_effects=True),
        name="intersect",
    )(old_proj, new_proj)


def moved(packed, operands, shift_mask):
    experts = lax.axis_size("expert")

    def leaf(mask):
        pairs = [(source, source ^ mask) for source in range(experts)]

        def branch(array, inputs):
            return (lax.ppermute(array, "expert", pairs),) + tuple(exchanged(*inputs))

        return branch

    def tree(low, high):
        if high - low == 1:
            return leaf(low)
        middle = (low + high) // 2
        below, above = tree(low, middle), tree(middle, high)
        return lambda array, inputs: lax.cond(
            shift_mask < middle, below, above, array, inputs
        )

    return tree(1, experts)(packed, operands)


def per_device(
    weight,
    first_moment,
    second_moment,
    projector_old,
    projector_new,
    change_flag,
    partner,
    hidden_act,
    out_grad,
    route,
):
    own_index = lax.axis_index("expert")
    shift_mask = partner[0]
    changed = change_flag[own_index] > 0
    old_proj, new_proj = projector_old[0], projector_new[0]
    active_home = jnp.where(changed, new_proj, old_proj)
    intersection = intersection_of(old_proj, new_proj)
    first_turned = jnp.dot(first_moment[0], intersection, precision=lax.Precision.HIGHEST)
    second_turned = jnp.dot(
        second_moment[0], intersection * intersection, precision=lax.Precision.HIGHEST
    )
    first_start = jnp.where(changed, first_turned, first_moment[0]).astype(jnp.bfloat16)
    second_start = jnp.where(changed, second_turned, second_moment[0]).astype(jnp.bfloat16)

    home = route[:, 0]
    columns = jnp.arange(EX, dtype=jnp.int32)
    picked = (home[:, None] == columns[None, :]).astype(jnp.int32)
    rank_of = jnp.sum((jnp.cumsum(picked, axis=0) - picked) * picked, axis=1)
    tokens = home.shape[0]
    pos_home = jnp.broadcast_to((home * CAP + rank_of)[None, :], (8, tokens))
    pos_target = jnp.broadcast_to(
        (jnp.bitwise_xor(home, shift_mask) * CAP + rank_of)[None, :], (8, tokens)
    )
    act4 = jnp.stack(
        [
            active_home[0:256],
            active_home[256:512],
            active_home[512:768],
            jnp.concatenate([jnp.zeros_like(active_home[:128]), active_home[768:896]], axis=0),
        ]
    )
    packed, proj_grad, projector_full = moved(
        jnp.concatenate([weight[0], first_start, second_start], axis=1),
        (partner[:1], out_grad, hidden_act, act4, pos_home, pos_target),
        shift_mask,
    )
    width, rank = weight.shape[2], first_start.shape[1]
    weight_here = packed[:, :width]
    first_start = packed[:, width : width + rank]
    second_start = packed[:, width + rank :]
    first_next = beta_one * first_start.astype(jnp.float32) + (1.0 - beta_one) * proj_grad
    second_next = (
        beta_two * second_start.astype(jnp.float32) + (1.0 - beta_two) * proj_grad * proj_grad
    )
    direction = (first_next / (jnp.sqrt(second_next) + adam_eps)).astype(jnp.bfloat16)
    update = lax.dot_general(
        direction, projector_full, (((1,), (1,)), ((), ())), preferred_element_type=jnp.float32
    )
    new_weight = (weight_here.astype(jnp.float32) - step_size * update).astype(jnp.bfloat16)
    rows = active_home.shape[0]
    active = lax.dynamic_slice_in_dim(projector_full, lax.axis_index("dp") * rows, rows, 0)
    return (new_weight[None], first_next[None], second_next[None], active[None])


def solution(mesh):
    in_specs = (
        P("expert", "dp", None),
        P("expert", "dp", None),
        P("expert", "dp", None),
        P("expert", "dp", None),
        P("expert", "dp", None),
        P(),
        P(),
        P(("dp", "expert"), None),
        P(("dp", "expert"), None),
        P(("dp", "expert"), None),
    )
    out_specs = (
        P("expert", "dp", None),
        P("expert", "dp", None),
        P("expert", "dp", None),
        P("expert", "dp", None),
    )
    return jax.shard_map(
        per_device, mesh=mesh, in_specs=in_specs, out_specs=out_specs, check_vma=False
    )
```

```python
import jax
import jax.numpy as jnp
from jax import lax
from jax.experimental import pallas as pl
from jax.experimental.pallas import tpu as pltpu
from jax.sharding import PartitionSpec as P

beta_one = 0.9
beta_two = 0.95
adam_eps = 1e-08
step_size = 2.0

NX, NY, NZ = 4, 4, 8
EX = NX * NZ
CAP = 16
SLOTS = EX * CAP
WIDTH = 7168
PEERS = NX * NY
HALF = NZ // 2
MESH = pl.DeviceIdType.MESH
CONTRACT_ROWS = (((0,), (0,)), ((), ()))


def one_hot(pos_row, first=0, count=SLOTS):
    slot = first + lax.broadcasted_iota(jnp.int32, (count, pos_row.shape[1]), 0)
    return jnp.where(slot == pos_row, 1.0, 0.0).astype(jnp.bfloat16)


def project_kernel(
    c_ref,
    grad,
    hidden,
    act4,
    pos_home,
    pos_target,
    old,
    new,
    y_out,
    sel_out,
    h_recv,
    inter_out,
    tok,
    pos_all,
    proj,
    srt,
    alg,
    h_send,
    parts,
    landed,
    summed,
    loc_sem,
    xs_sem,
    xr_sem,
    ts_sem,
    tr_sem,
    ps_sem,
    pr_sem,
    rs_sem,
    rr_sem,
    ls_sem,
    lr_sem,
    ss_sem,
    sr_sem,
    hs_sem,
    hr_sem,
    is_sem,
    ir_sem,
    ws_sem,
    wr_sem,
):
    d = lax.axis_index("dp")
    e = lax.axis_index("expert")
    x, z = e // NZ, e % NZ
    y, core = d // 2, d % 2
    me = x * NY + y
    tokens = hidden.shape[0]
    rows = grad.shape[1] // (2 * NY)
    sibling = (2 * y + 1 - core, e)

    def plane(k):
        px, py = (x + k % NX) % NX, (y + k // NX) % NY
        return px, py, (2 * py + core, px * NZ + z)

    def plane_from(k):
        px, py = (x + NX - k % NX) % NX, (y + NY - k // NX) % NY
        return px * NY + py

    def remote(src, dst, send, recv, device):
        return pltpu.make_async_remote_copy(
            src, dst, send, recv, device_id=device, device_id_type=MESH
        )

    def repeat(low, high, do):
        def step(k, carry):
            do(k)
            return carry

        lax.fori_loop(low, high, step, 0)

    def settle(view, sem):
        pltpu.make_async_copy(view, view, sem).wait()

    drain = []
    barrier = pltpu.get_barrier_semaphore()
    group = 2 * NY
    share = parts.shape[1]

    def dp_peer(k):
        return (d + k) % group

    def part_copy(k):
        to = dp_peer(k)
        return remote(parts.at[to], landed.at[d], is_sem, ir_sem, (to, e))

    def share_copy(k):
        own = inter_out.at[pl.ds(pl.multiple_of(d * share, share), share)]
        return remote(summed, own, ws_sem, wr_sem, (dp_peer(k), e))


    def greet(device):
        pl.semaphore_signal(barrier, inc=1, device_id=device, device_id_type=MESH)

    repeat(1, EX, lambda k: greet((d, (e + k) % EX)))
    repeat(NX, PEERS, lambda k: greet(plane(k)[2]))
    repeat(0, NY, lambda k: greet((2 * ((y + k) % NY) + 1 - core, e)))
    local = lax.dot_general(
        old[...], new[...], CONTRACT_ROWS, preferred_element_type=jnp.float32
    )
    for part in range(group):
        parts[part] = local[part * share : (part + 1) * share]
    pl.semaphore_wait(barrier, EX - 1 + PEERS - NX + NY)

    mine = pl.ds(pl.multiple_of(core * 256, 256), 256)

    def proj_copy(k):
        px = (x + k) % NX
        return remote(
            act4.at[px], proj.at[x, z, mine], xs_sem, xr_sem, (d, px * NZ + z)
        )

    def columns(px, py, part):
        start = (2 * py + part) * rows + (2 * px - px // 3) * 128
        return pl.ds(pl.multiple_of(start, 128), 256)

    def tok_copy(k, part):
        px, py, device = plane(k)
        return remote(
            grad.at[:, columns(px, py, part)],
            tok.at[me, :, pl.ds(part * 256, 256)],
            ts_sem,
            tr_sem.at[me],
            device,
        )

    def pos_copy(k):
        return remote(pos_home, pos_all.at[me], ps_sem, pr_sem.at[me], plane(k)[2])

    for k in range(1, NX):
        proj_copy(k).start()
    drain.append((act4.at[pl.ds(0, NX - 1)], xs_sem))
    for k in range(1, group):
        part_copy(k).start()
    drain.append((landed.at[pl.ds(0, group - 1)], is_sem))
    landed[d] = parts[d]
    own_proj = pltpu.make_async_copy(act4.at[x], proj.at[x, z, mine], loc_sem.at[0])
    own_proj.start()
    repeat(1, PEERS, lambda k: pos_copy(k).start())
    drain.append((pos_all.at[pl.ds(0, PEERS - 1)], ps_sem))

    def start_tok(k):
        tok_copy(k, 0).start()
        tok_copy(k, 1).start()

    repeat(1, PEERS, start_tok)
    drain.append((tok.at[pl.ds(0, PEERS - 1)], ts_sem))
    own_tok = [
        pltpu.make_async_copy(
            grad.at[:, columns(x, y, part)],
            tok.at[me, :, pl.ds(part * 256, 256)],
            loc_sem.at[1 + part],
        )
        for part in range(2)
    ]
    for copy in own_tok:
        copy.start()
    pos_all[me] = pos_home[...]

    def sort_hidden(i):
        chunk = pl.ds(pl.multiple_of(i * 64, 64), 64)
        h_send[chunk] = jnp.dot(
            one_hot(pos_target[0:1], i * 64, 64),
            hidden[...],
            preferred_element_type=jnp.float32,
        ).astype(jnp.bfloat16)

    repeat(0, SLOTS // 64, sort_hidden)

    settle(landed.at[pl.ds(0, group - 1)], ir_sem)
    summed[...] = jnp.sum(landed[...], axis=0)
    for k in range(1, group):
        share_copy(k).start()
    drain.append((landed.at[pl.ds(0, group - 1)], ws_sem))
    inter_out[pl.ds(pl.multiple_of(d * share, share), share)] = summed[...]
    own_proj.wait()
    settle(proj.at[pl.ds(0, NX - 1), 0, pl.ds(0, 256)], xr_sem)

    def ring_copy(step, right):
        if right:
            zz, to, send, recv = (z + NZ - step + 1) % NZ, (z + 1) % NZ, rs_sem, rr_sem
        else:
            zz, to, send, recv = (z + step - 1) % NZ, (z + NZ - 1) % NZ, ls_sem, lr_sem
        xs = pl.ds(0, NX)
        if step == HALF:
            xs = pl.ds(0 if right else NX // 2, NX // 2)
        view = proj.at[xs, zz, mine]
        return remote(view, view, send.at[step - 1], recv.at[step - 1], (d, x * NZ + to))

    def sib_copy(zz):
        view = proj.at[:, zz, mine]
        return remote(view, view, ss_sem.at[zz], sr_sem.at[zz], sibling)

    def ring_drain():
        for step in range(1, HALF + 1):
            ring_copy(step, True).wait_send()
            ring_copy(step, False).wait_send()
        repeat(0, NZ, lambda k: sib_copy(k).wait_send())

    def sort_block(k):
        slot = plane_from(k)
        settle(tok.at[slot], tr_sem.at[slot])
        settle(pos_all.at[slot], pr_sem.at[slot])
        sort_slot(slot)

    def sort_slot(slot):
        rows_of = pl.ds(pl.multiple_of(slot * CAP, CAP), CAP)

        def sort_part(i):
            sorted_rows = jnp.dot(
                one_hot(pos_all[slot, 0:1], i * 8 * CAP, 8 * CAP),
                tok[slot],
                preferred_element_type=jnp.float32,
            ).astype(jnp.bfloat16)
            srt[pl.ds(i * 8, 8), rows_of, :] = sorted_rows.reshape(8, CAP, 512)

        repeat(0, EX // 8, sort_part)

    def hid_copy(k):
        to = (e + k) % EX
        return remote(
            h_send.at[pl.ds(pl.multiple_of(to * CAP, CAP), CAP)],
            h_recv.at[pl.ds(pl.multiple_of(e * CAP, CAP), CAP)],
            hs_sem,
            hr_sem,
            (d, to),
        )

    ring_copy(1, True).start()
    ring_copy(1, False).start()
    sib_copy(z).start()
    for copy in own_tok:
        copy.wait()
    sort_slot(me)
    bounds = [1, 3, 6, 9, 11]
    others = pl.ds(0, SLOTS - CAP)
    for step in range(1, HALF + 1):
        repeat(bounds[step - 1], bounds[step], sort_block)
        ring_copy(step, True).wait_recv()
        if step < HALF:
            ring_copy(step + 1, True).start()
        ring_copy(step, False).wait_recv()
        if step < HALF:
            ring_copy(step + 1, False).start()
            sib_copy((z + NZ - step) % NZ).start()
            sib_copy((z + step) % NZ).start()
        else:
            sib_copy((z + HALF) % NZ).start()
        if step == HALF - 1:
            repeat(1, EX, lambda k: hid_copy(k).start())
            drain.append((h_send.at[others], hs_sem))
    repeat(bounds[HALF], PEERS, sort_block)
    repeat(0, NZ, lambda k: sib_copy(k).wait_recv())

    own_rows = pl.ds(pl.multiple_of(e * CAP, CAP), CAP)
    h_recv[own_rows] = h_send[own_rows]

    def multiply(index):
        alg[index] = jnp.dot(
            srt[index], proj[index // NZ, index % NZ], preferred_element_type=jnp.float32
        ).astype(jnp.bfloat16)

    repeat(0, EX, multiply)

    def unsorted(slot):
        block = alg[:, pl.ds(pl.multiple_of(slot * CAP, CAP), CAP), :].reshape(SLOTS, 256)
        return lax.dot_general(
            one_hot(pos_all[slot, 0:1]),
            block,
            CONTRACT_ROWS,
            preferred_element_type=jnp.float32,
        ).astype(jnp.bfloat16)

    def keep_unsorted(slot):
        y_out[slot] = unsorted(slot)

    repeat(0, PEERS, keep_unsorted)
    shift = c_ref[0]
    for px in range(NX):
        from_expert = jnp.bitwise_xor(px * NZ + z, shift)
        sel_out[px] = proj[from_expert // NZ, from_expert % NZ, mine, :]
    settle(h_recv.at[others], hr_sem)
    settle(inter_out.at[pl.ds(0, (group - 1) * share)], wr_sem)
    ring_drain()
    for view, sem in drain:
        settle(view, sem)


def combine_kernel(
    y_send,
    sel,
    h_recv,
    pos_target,
    pg_out,
    full_out,
    y_recv,
    a_send,
    a_recv,
    p_send,
    p_recv,
    total,
    loc_sem,
    ys_sem,
    yr_sem,
    as_sem,
    ar_sem,
    gs_sem,
    gr_sem,
    ns_sem,
    nr_sem,
    fs_sem,
    fr_sem,
    us_sem,
    ur_sem,
):
    d = lax.axis_index("dp")
    e = lax.axis_index("expert")
    x, z = e // NZ, e % NZ
    y, core = d // 2, d % 2
    me = x * NY + y
    tokens = pos_target.shape[1]
    rows = full_out.shape[0] // (2 * NY)
    sibling = (2 * y + 1 - core, e)

    def plane(k):
        px, py = (x + k % NX) % NX, (y + k // NX) % NY
        return px, py, (2 * py + core, px * NZ + z)

    def plane_from(k):
        px, py = (x + NX - k % NX) % NX, (y + NY - k // NX) % NY
        return px * NY + py

    def remote(src, dst, send, recv, device):
        return pltpu.make_async_remote_copy(
            src, dst, send, recv, device_id=device, device_id_type=MESH
        )

    def repeat(low, high, do):
        def step(k, carry):
            do(k)
            return carry

        lax.fori_loop(low, high, step, 0)

    def settle(view, sem):
        pltpu.make_async_copy(view, view, sem).wait()

    drain = []
    barrier = pltpu.get_barrier_semaphore()

    def greet(device):
        pl.semaphore_signal(barrier, inc=1, device_id=device, device_id_type=MESH)

    repeat(1, EX, lambda k: greet((d, (e + k) % EX)))
    repeat(NX, PEERS, lambda k: greet(plane(k)[2]))
    repeat(0, NY, lambda k: greet((2 * ((y + k) % NY) + 1 - core, e)))
    pl.semaphore_wait(barrier, EX - 1 + PEERS - NX + NY)
    others = pl.ds(0, SLOTS - CAP)
    own_rows = pl.ds(pl.multiple_of(e * CAP, CAP), CAP)

    def y_copy(k):
        px, py, device = plane(k)
        return remote(y_send.at[px * NY + py], y_recv.at[me], ys_sem, yr_sem, device)

    repeat(1, PEERS, lambda k: y_copy(k).start())
    drain.append((y_send.at[pl.ds(0, PEERS - 1)], ys_sem))
    y_recv[me] = y_send[me]

    def sel_copy(px, last):
        size = 128 if last else 256
        off = 128 if last else 0
        dst = full_out.at[pl.ds(pl.multiple_of(d * rows + x * 256, 128), size)]
        return sel.at[px, pl.ds(off, size)], dst

    def sel_start(last):
        for k in range(1, NX):
            px = (x + k) % NX
            src, dst = sel_copy(px, last)
            remote(src, dst, ns_sem, nr_sem, (d, px * NZ + z)).start()
        src, dst = sel_copy(x, last)
        own = pltpu.make_async_copy(src, dst, loc_sem)
        own.start()
        own.wait()

    @pl.when(x < NX - 1)
    def _():
        sel_start(False)

    @pl.when(x == NX - 1)
    def _():
        sel_start(True)

    def sel_settle():
        @pl.when(x < NX - 1)
        def _():
            settle(full_out.at[pl.ds(0, rows - 256)], nr_sem)
            settle(sel.at[pl.ds(0, NX - 1)], ns_sem)

        @pl.when(x == NX - 1)
        def _():
            settle(full_out.at[pl.ds(0, rows - 128)], nr_sem)
            settle(sel.at[pl.ds(0, NX - 1), pl.ds(0, 128)], ns_sem)

    sel_settle()

    def full_rows(which):
        return full_out.at[pl.ds(pl.multiple_of(which * rows, 128), rows)]

    def full_copy(k):
        py = (y + k) % NY
        return remote(
            full_rows(d), full_rows(d), fs_sem, fr_sem.at[k], (2 * py + core, e)
        )

    def up_copy(k):
        view = full_rows(2 * ((y + NY - k) % NY) + core)
        return remote(view, view, us_sem, ur_sem, sibling)

    for k in range(1, NY):
        full_copy(k).start()
    up_copy(0).start()
    drain.append((full_out.at[pl.ds(0, (NY - 1) * rows)], fs_sem))
    drain.append((full_out.at[pl.ds(0, NY * rows)], us_sem))
    drain.append((full_out.at[pl.ds(0, NY * rows)], ur_sem))

    def up_rest():
        for k in range(1, NY):
            full_copy(k).wait_recv()
            up_copy(k).start()

    settle(y_recv.at[pl.ds(0, PEERS - 1)], yr_sem)

    def add_up(i):
        chunk = pl.ds(pl.multiple_of(i * 32, 32), 32)
        total[chunk] = jnp.sum(y_recv[:, chunk, :].astype(jnp.float32), axis=0).astype(
            jnp.bfloat16
        )

    repeat(0, tokens // 32, add_up)

    def sort_total(i):
        chunk = pl.ds(pl.multiple_of(i * 128, 128), 128)
        a_send[chunk] = jnp.dot(
            one_hot(pos_target[0:1], i * 128, 128),
            total[...],
            preferred_element_type=jnp.float32,
        ).astype(jnp.bfloat16)

    repeat(0, SLOTS // 128, sort_total)

    def alg_copy(k):
        to = (e + k) % EX
        return remote(
            a_send.at[pl.ds(pl.multiple_of(to * CAP, CAP), CAP)],
            a_recv.at[pl.ds(pl.multiple_of(e * CAP, CAP), CAP)],
            as_sem,
            ar_sem,
            (d, to),
        )

    repeat(1, EX, lambda k: alg_copy(k).start())
    drain.append((a_send.at[others], as_sem))
    a_recv[own_rows] = a_send[own_rows]
    settle(a_recv.at[others], ar_sem)

    ff = p_send.shape[1]

    def outer(part):
        p_send[part] = lax.dot_general(
            h_recv[:, pl.ds(pl.multiple_of(part * ff, ff), ff)],
            a_recv[...],
            CONTRACT_ROWS,
            preferred_element_type=jnp.float32,
        ).astype(jnp.bfloat16)

    repeat(0, 2 * NY, outer)

    def pg_copy(k):
        to = (d + k) % (2 * NY)
        return remote(p_send.at[to], p_recv.at[d], gs_sem, gr_sem, (to, e))

    repeat(1, 2 * NY, lambda k: pg_copy(k).start())
    drain.append((p_send.at[pl.ds(0, 2 * NY - 1)], gs_sem))
    p_recv[d] = p_send[d]
    up_rest()
    settle(p_recv.at[pl.ds(0, 2 * NY - 1)], gr_sem)

    def finish(i):
        chunk = pl.ds(pl.multiple_of(i * 32, 32), 32)
        pg_out[chunk] = jnp.sum(p_recv[:, chunk, :].astype(jnp.float32), axis=0)

    repeat(0, ff // 32, finish)

    for view, sem in drain:
        settle(view, sem)


def projected(shift_mask, grad, hidden, act4, pos_home, pos_target, old, new):
    tokens, width = grad.shape
    ff = hidden.shape[1]
    rank = act4.shape[2]
    share = rank // (2 * NY)
    bf16, f32 = jnp.bfloat16, jnp.float32
    vmem = pl.BlockSpec(memory_space=pltpu.VMEM)
    hbm = pl.BlockSpec(memory_space=pl.ANY)
    dma = pltpu.SemaphoreType.DMA
    return pl.pallas_call(
        project_kernel,
        out_shape=(
            jax.ShapeDtypeStruct((PEERS, tokens, rank), bf16),
            jax.ShapeDtypeStruct((NX, 256, rank), bf16),
            jax.ShapeDtypeStruct((SLOTS, ff), bf16),
            jax.ShapeDtypeStruct((rank, rank), f32),
        ),
        in_specs=[pl.BlockSpec(memory_space=pltpu.SMEM), hbm] + [vmem] * 6,
        out_specs=(vmem,) * 4,
        scratch_shapes=[
            pltpu.VMEM((PEERS, tokens, 512), bf16),
            pltpu.VMEM((PEERS, 8, tokens), jnp.int32),
            pltpu.VMEM((NX, NZ, 512, rank), bf16),
            pltpu.VMEM((EX, PEERS * CAP, 512), bf16),
            pltpu.VMEM((EX, PEERS * CAP, rank), bf16),
            pltpu.VMEM((SLOTS, ff), bf16),
            pltpu.VMEM((2 * NY, share, rank), f32),
            pltpu.VMEM((2 * NY, share, rank), f32),
            pltpu.VMEM((share, rank), f32),
            dma((3,)),
            dma,
            dma,
            dma,
            dma((PEERS,)),
            dma,
            dma((PEERS,)),
            dma((HALF,)),
            dma((HALF,)),
            dma((HALF,)),
            dma((HALF,)),
            dma((NZ,)),
            dma((NZ,)),
            dma,
            dma,
            dma,
            dma,
            dma,
            dma,
        ],
        compiler_params=pltpu.CompilerParams(
            collective_id=0, has_side_effects=True, vmem_limit_bytes=60 * 1024 * 1024
        ),
        name="project_tokens",
    )(shift_mask, grad, hidden, act4, pos_home, pos_target, old, new)


def combined(y_parts, sel, hidden_rows, pos_target):
    peers, tokens, rank = y_parts.shape
    ff = hidden_rows.shape[1]
    group = 2 * NY
    bf16 = jnp.bfloat16
    vmem = pl.BlockSpec(memory_space=pltpu.VMEM)
    hbm = pl.BlockSpec(memory_space=pl.ANY)
    dma = pltpu.SemaphoreType.DMA
    return pl.pallas_call(
        combine_kernel,
        out_shape=(
            jax.ShapeDtypeStruct((ff // group, rank), jnp.float32),
            jax.ShapeDtypeStruct((WIDTH, rank), bf16),
        ),
        in_specs=[vmem] * 4,
        out_specs=(vmem, hbm),
        scratch_shapes=[
            pltpu.VMEM((PEERS, tokens, rank), bf16),
            pltpu.VMEM((SLOTS, rank), bf16),
            pltpu.VMEM((SLOTS, rank), bf16),
            pltpu.VMEM((group, ff // group, rank), bf16),
            pltpu.VMEM((group, ff // group, rank), bf16),
            pltpu.VMEM((tokens, rank), bf16),
            dma,
            dma,
            dma,
            dma,
            dma,
            dma,
            dma,
            dma,
            dma,
            dma,
            dma((NY,)),
            dma,
            dma,
        ],
        compiler_params=pltpu.CompilerParams(
            collective_id=1, has_side_effects=True, vmem_limit_bytes=48 * 1024 * 1024
        ),
        cost_estimate=pl.CostEstimate(
            flops=1_000_000_000, bytes_accessed=300_000_000, transcendentals=0
        ),
        name="combine_rows",
    )(y_parts, sel, hidden_rows, pos_target)


def moved(packed, operands, shift_mask):
    experts = lax.axis_size("expert")

    def leaf(mask):
        pairs = [(source, source ^ mask) for source in range(experts)]

        def branch(array, inputs):
            return (lax.ppermute(array, "expert", pairs),) + tuple(combined(*inputs))

        return branch

    def tree(low, high):
        if high - low == 1:
            return leaf(low)
        middle = (low + high) // 2
        below, above = tree(low, middle), tree(middle, high)
        return lambda array, inputs: lax.cond(
            shift_mask < middle, below, above, array, inputs
        )

    return tree(1, experts)(packed, operands)


def per_device(
    weight,
    first_moment,
    second_moment,
    projector_old,
    projector_new,
    change_flag,
    partner,
    hidden_act,
    out_grad,
    route,
):
    own_index = lax.axis_index("expert")
    shift_mask = partner[0]
    changed = change_flag[own_index] > 0
    old_proj, new_proj = projector_old[0], projector_new[0]
    active_home = jnp.where(changed, new_proj, old_proj)
    home = route[:, 0]
    columns = jnp.arange(EX, dtype=jnp.int32)
    picked = (home[:, None] == columns[None, :]).astype(jnp.int32)
    rank_of = jnp.sum((jnp.cumsum(picked, axis=0) - picked) * picked, axis=1)
    tokens = home.shape[0]
    pos_home = jnp.broadcast_to((home * CAP + rank_of)[None, :], (8, tokens))
    pos_target = jnp.broadcast_to(
        (jnp.bitwise_xor(home, shift_mask) * CAP + rank_of)[None, :], (8, tokens)
    )
    act4 = jnp.stack(
        [
            active_home[0:256],
            active_home[256:512],
            active_home[512:768],
            jnp.concatenate([jnp.zeros_like(active_home[:128]), active_home[768:896]], axis=0),
        ]
    )
    y_parts, sel, hidden_rows, intersection = projected(
        partner[:1], out_grad, hidden_act, act4, pos_home, pos_target, old_proj, new_proj
    )
    first_turned = jnp.dot(first_moment[0], intersection, precision=lax.Precision.HIGHEST)
    second_turned = jnp.dot(
        second_moment[0], intersection * intersection, precision=lax.Precision.HIGHEST
    )
    first_start = jnp.where(changed, first_turned, first_moment[0]).astype(jnp.bfloat16)
    second_start = jnp.where(changed, second_turned, second_moment[0]).astype(jnp.bfloat16)
    packed, proj_grad, projector_full = moved(
        jnp.concatenate([weight[0], first_start, second_start], axis=1),
        (y_parts, sel, hidden_rows, pos_target),
        shift_mask,
    )
    width, rank = weight.shape[2], first_start.shape[1]
    weight_here = packed[:, :width]
    first_start = packed[:, width : width + rank]
    second_start = packed[:, width + rank :]
    first_next = beta_one * first_start.astype(jnp.float32) + (1.0 - beta_one) * proj_grad
    second_next = (
        beta_two * second_start.astype(jnp.float32) + (1.0 - beta_two) * proj_grad * proj_grad
    )
    direction = (first_next / (jnp.sqrt(second_next) + adam_eps)).astype(jnp.bfloat16)
    update = lax.dot_general(
        direction, projector_full, (((1,), (1,)), ((), ())), preferred_element_type=jnp.float32
    )
    new_weight = (weight_here.astype(jnp.float32) - step_size * update).astype(jnp.bfloat16)
    rows = active_home.shape[0]
    active = lax.dynamic_slice_in_dim(projector_full, lax.axis_index("dp") * rows, rows, 0)
    return (new_weight[None], first_next[None], second_next[None], active[None])


def solution(mesh):
    in_specs = (
        P("expert", "dp", None),
        P("expert", "dp", None),
        P("expert", "dp", None),
        P("expert", "dp", None),
        P("expert", "dp", None),
        P(),
        P(),
        P(("dp", "expert"), None),
        P(("dp", "expert"), None),
        P(("dp", "expert"), None),
    )
    out_specs = (
        P("expert", "dp", None),
        P("expert", "dp", None),
        P("expert", "dp", None),
        P("expert", "dp", None),
    )
    return jax.shard_map(
        per_device, mesh=mesh, in_specs=in_specs, out_specs=out_specs, check_vma=False
    )
```

```python
import jax
import jax.numpy as jnp
from jax import lax
from jax.experimental import pallas as pl
from jax.experimental.pallas import tpu as pltpu
from jax.sharding import PartitionSpec as P

beta_one = 0.9
beta_two = 0.95
adam_eps = 1e-08
step_size = 2.0

NX, NY, NZ = 4, 4, 8
EX = NX * NZ
CAP = 16
SLOTS = EX * CAP
WIDTH = 7168
PEERS = NX * NY
HALF = NZ // 2
MESH = pl.DeviceIdType.MESH
CONTRACT_ROWS = (((0,), (0,)), ((), ()))


def one_hot(pos_row, first=0, count=SLOTS):
    slot = first + lax.broadcasted_iota(jnp.int32, (count, pos_row.shape[1]), 0)
    return jnp.where(slot == pos_row, 1.0, 0.0).astype(jnp.bfloat16)


def project_kernel(
    c_ref,
    grad,
    hidden,
    act4,
    pos_home,
    pos_target,
    old,
    new,
    y_out,
    np_out,
    h_recv,
    inter_out,
    tok,
    pos_all,
    proj,
    srt,
    alg,
    h_send,
    sel,
    parts,
    landed,
    summed,
    loc_sem,
    xs_sem,
    xr_sem,
    ts_sem,
    tr_sem,
    ps_sem,
    pr_sem,
    rs_sem,
    rr_sem,
    ls_sem,
    lr_sem,
    ss_sem,
    sr_sem,
    hs_sem,
    hr_sem,
    is_sem,
    ir_sem,
    ws_sem,
    wr_sem,
    ns_sem,
    nr_sem,
):
    d = lax.axis_index("dp")
    e = lax.axis_index("expert")
    x, z = e // NZ, e % NZ
    y, core = d // 2, d % 2
    me = x * NY + y
    tokens = hidden.shape[0]
    rows = grad.shape[1] // (2 * NY)
    sibling = (2 * y + 1 - core, e)

    def plane(k):
        px, py = (x + k % NX) % NX, (y + k // NX) % NY
        return px, py, (2 * py + core, px * NZ + z)

    def plane_from(k):
        px, py = (x + NX - k % NX) % NX, (y + NY - k // NX) % NY
        return px * NY + py

    def remote(src, dst, send, recv, device):
        return pltpu.make_async_remote_copy(
            src, dst, send, recv, device_id=device, device_id_type=MESH
        )

    def repeat(low, high, do):
        def step(k, carry):
            do(k)
            return carry

        lax.fori_loop(low, high, step, 0)

    def settle(view, sem):
        pltpu.make_async_copy(view, view, sem).wait()

    drain = []
    barrier = pltpu.get_barrier_semaphore()
    group = 2 * NY
    share = parts.shape[1]

    def dp_peer(k):
        return (d + k) % group

    def part_copy(k):
        to = dp_peer(k)
        return remote(parts.at[to], landed.at[d], is_sem, ir_sem, (to, e))

    def share_copy(k):
        own = inter_out.at[pl.ds(pl.multiple_of(d * share, share), share)]
        return remote(summed, own, ws_sem, wr_sem, (dp_peer(k), e))


    def greet(device):
        pl.semaphore_signal(barrier, inc=1, device_id=device, device_id_type=MESH)

    repeat(1, EX, lambda k: greet((d, (e + k) % EX)))
    repeat(NX, PEERS, lambda k: greet(plane(k)[2]))
    repeat(0, NY, lambda k: greet((2 * ((y + k) % NY) + 1 - core, e)))
    local = lax.dot_general(
        old[...], new[...], CONTRACT_ROWS, preferred_element_type=jnp.float32
    )
    for part in range(group):
        parts[part] = local[part * share : (part + 1) * share]
    pl.semaphore_wait(barrier, EX - 1 + PEERS - NX + NY)

    mine = pl.ds(pl.multiple_of(core * 256, 256), 256)

    def proj_copy(k):
        px = (x + k) % NX
        return remote(
            act4.at[px], proj.at[x, z, mine], xs_sem, xr_sem, (d, px * NZ + z)
        )

    def columns(px, py, part):
        start = (2 * py + part) * rows + (2 * px - px // 3) * 128
        return pl.ds(pl.multiple_of(start, 128), 256)

    def tok_copy(k, part):
        px, py, device = plane(k)
        return remote(
            grad.at[:, columns(px, py, part)],
            tok.at[me, :, pl.ds(part * 256, 256)],
            ts_sem,
            tr_sem.at[me],
            device,
        )

    def pos_copy(k):
        return remote(pos_home, pos_all.at[me], ps_sem, pr_sem.at[me], plane(k)[2])

    for k in range(1, NX):
        proj_copy(k).start()
    drain.append((act4.at[pl.ds(0, NX - 1)], xs_sem))
    for k in range(1, group):
        part_copy(k).start()
    drain.append((landed.at[pl.ds(0, group - 1)], is_sem))
    landed[d] = parts[d]
    own_proj = pltpu.make_async_copy(act4.at[x], proj.at[x, z, mine], loc_sem.at[0])
    own_proj.start()
    repeat(1, PEERS, lambda k: pos_copy(k).start())
    drain.append((pos_all.at[pl.ds(0, PEERS - 1)], ps_sem))

    def start_tok(k):
        tok_copy(k, 0).start()
        tok_copy(k, 1).start()

    repeat(1, PEERS, start_tok)
    drain.append((tok.at[pl.ds(0, PEERS - 1)], ts_sem))
    own_tok = [
        pltpu.make_async_copy(
            grad.at[:, columns(x, y, part)],
            tok.at[me, :, pl.ds(part * 256, 256)],
            loc_sem.at[1 + part],
        )
        for part in range(2)
    ]
    for copy in own_tok:
        copy.start()
    pos_all[me] = pos_home[...]

    def sort_hidden(i):
        chunk = pl.ds(pl.multiple_of(i * 64, 64), 64)
        h_send[chunk] = jnp.dot(
            one_hot(pos_target[0:1], i * 64, 64),
            hidden[...],
            preferred_element_type=jnp.float32,
        ).astype(jnp.bfloat16)

    repeat(0, SLOTS // 64, sort_hidden)

    settle(landed.at[pl.ds(0, group - 1)], ir_sem)
    summed[...] = jnp.sum(landed[...], axis=0)
    for k in range(1, group):
        share_copy(k).start()
    drain.append((landed.at[pl.ds(0, group - 1)], ws_sem))
    inter_out[pl.ds(pl.multiple_of(d * share, share), share)] = summed[...]
    own_proj.wait()
    settle(proj.at[pl.ds(0, NX - 1), 0, pl.ds(0, 256)], xr_sem)

    def ring_copy(step, right):
        if right:
            zz, to, send, recv = (z + NZ - step + 1) % NZ, (z + 1) % NZ, rs_sem, rr_sem
        else:
            zz, to, send, recv = (z + step - 1) % NZ, (z + NZ - 1) % NZ, ls_sem, lr_sem
        xs = pl.ds(0, NX)
        if step == HALF:
            xs = pl.ds(0 if right else NX // 2, NX // 2)
        view = proj.at[xs, zz, mine]
        return remote(view, view, send.at[step - 1], recv.at[step - 1], (d, x * NZ + to))

    def sib_copy(zz):
        view = proj.at[:, zz, mine]
        return remote(view, view, ss_sem.at[zz], sr_sem.at[zz], sibling)

    def ring_drain():
        for step in range(1, HALF + 1):
            ring_copy(step, True).wait_send()
            ring_copy(step, False).wait_send()
        repeat(0, NZ, lambda k: sib_copy(k).wait_send())

    def sort_block(k):
        slot = plane_from(k)
        settle(tok.at[slot], tr_sem.at[slot])
        settle(pos_all.at[slot], pr_sem.at[slot])
        sort_slot(slot)

    def sort_slot(slot):
        rows_of = pl.ds(pl.multiple_of(slot * CAP, CAP), CAP)

        def sort_part(i):
            sorted_rows = jnp.dot(
                one_hot(pos_all[slot, 0:1], i * 8 * CAP, 8 * CAP),
                tok[slot],
                preferred_element_type=jnp.float32,
            ).astype(jnp.bfloat16)
            srt[pl.ds(i * 8, 8), rows_of, :] = sorted_rows.reshape(8, CAP, 512)

        repeat(0, EX // 8, sort_part)

    def hid_copy(k):
        to = (e + k) % EX
        return remote(
            h_send.at[pl.ds(pl.multiple_of(to * CAP, CAP), CAP)],
            h_recv.at[pl.ds(pl.multiple_of(e * CAP, CAP), CAP)],
            hs_sem,
            hr_sem,
            (d, to),
        )

    ring_copy(1, True).start()
    ring_copy(1, False).start()
    sib_copy(z).start()
    for copy in own_tok:
        copy.wait()
    sort_slot(me)
    bounds = [1, 3, 6, 9, 11]
    others = pl.ds(0, SLOTS - CAP)
    for step in range(1, HALF + 1):
        repeat(bounds[step - 1], bounds[step], sort_block)
        ring_copy(step, True).wait_recv()
        if step < HALF:
            ring_copy(step + 1, True).start()
        ring_copy(step, False).wait_recv()
        if step < HALF:
            ring_copy(step + 1, False).start()
            sib_copy((z + NZ - step) % NZ).start()
            sib_copy((z + step) % NZ).start()
        else:
            sib_copy((z + HALF) % NZ).start()
        if step == HALF - 1:
            repeat(1, EX, lambda k: hid_copy(k).start())
            drain.append((h_send.at[others], hs_sem))
    repeat(bounds[HALF], PEERS, sort_block)
    repeat(0, NZ, lambda k: sib_copy(k).wait_recv())

    own_rows = pl.ds(pl.multiple_of(e * CAP, CAP), CAP)
    h_recv[own_rows] = h_send[own_rows]

    shift = c_ref[0]
    for px in range(NX):
        from_expert = jnp.bitwise_xor(px * NZ + z, shift)
        sel[px] = proj[from_expert // NZ, from_expert % NZ, mine, :]

    def sel_copy(px, last):
        size = 128 if last else 256
        off = 128 if last else 0
        dst = np_out.at[pl.ds(pl.multiple_of(x * 256, 128), size)]
        return sel.at[px, pl.ds(off, size)], dst

    def sel_start(last):
        for k in range(1, NX):
            px = (x + k) % NX
            src, dst = sel_copy(px, last)
            remote(src, dst, ns_sem, nr_sem, (d, px * NZ + z)).start()
        src, dst = sel_copy(x, last)
        own = pltpu.make_async_copy(src, dst, loc_sem.at[3])
        own.start()
        own.wait()

    @pl.when(x < NX - 1)
    def _():
        sel_start(False)

    @pl.when(x == NX - 1)
    def _():
        sel_start(True)

    def multiply(index):
        alg[index] = jnp.dot(
            srt[index], proj[index // NZ, index % NZ], preferred_element_type=jnp.float32
        ).astype(jnp.bfloat16)

    repeat(0, EX, multiply)

    def unsorted(slot):
        block = alg[:, pl.ds(pl.multiple_of(slot * CAP, CAP), CAP), :].reshape(SLOTS, 256)
        return lax.dot_general(
            one_hot(pos_all[slot, 0:1]),
            block,
            CONTRACT_ROWS,
            preferred_element_type=jnp.float32,
        ).astype(jnp.bfloat16)

    def keep_unsorted(slot):
        y_out[slot] = unsorted(slot)

    repeat(0, PEERS, keep_unsorted)
    settle(h_recv.at[others], hr_sem)
    settle(inter_out.at[pl.ds(0, (group - 1) * share)], wr_sem)

    def sel_settle():
        @pl.when(x < NX - 1)
        def _():
            settle(np_out.at[pl.ds(0, rows - 256)], nr_sem)
            settle(sel.at[pl.ds(0, NX - 1)], ns_sem)

        @pl.when(x == NX - 1)
        def _():
            settle(np_out.at[pl.ds(0, rows - 128)], nr_sem)
            settle(sel.at[pl.ds(0, NX - 1), pl.ds(0, 128)], ns_sem)

    sel_settle()
    ring_drain()
    for view, sem in drain:
        settle(view, sem)


def combine_kernel(
    y_send,
    own_proj,
    h_recv,
    pos_target,
    pg_out,
    full_out,
    y_recv,
    a_send,
    a_recv,
    p_send,
    p_recv,
    total,
    loc_sem,
    ys_sem,
    yr_sem,
    as_sem,
    ar_sem,
    gs_sem,
    gr_sem,
    fs_sem,
    fr_sem,
    us_sem,
    ur_sem,
):
    d = lax.axis_index("dp")
    e = lax.axis_index("expert")
    x, z = e // NZ, e % NZ
    y, core = d // 2, d % 2
    me = x * NY + y
    tokens = pos_target.shape[1]
    rows = full_out.shape[0] // (2 * NY)
    sibling = (2 * y + 1 - core, e)

    def plane(k):
        px, py = (x + k % NX) % NX, (y + k // NX) % NY
        return px, py, (2 * py + core, px * NZ + z)

    def plane_from(k):
        px, py = (x + NX - k % NX) % NX, (y + NY - k // NX) % NY
        return px * NY + py

    def remote(src, dst, send, recv, device):
        return pltpu.make_async_remote_copy(
            src, dst, send, recv, device_id=device, device_id_type=MESH
        )

    def repeat(low, high, do):
        def step(k, carry):
            do(k)
            return carry

        lax.fori_loop(low, high, step, 0)

    def settle(view, sem):
        pltpu.make_async_copy(view, view, sem).wait()

    drain = []
    barrier = pltpu.get_barrier_semaphore()

    def greet(device):
        pl.semaphore_signal(barrier, inc=1, device_id=device, device_id_type=MESH)

    repeat(1, EX, lambda k: greet((d, (e + k) % EX)))
    repeat(NX, PEERS, lambda k: greet(plane(k)[2]))
    repeat(0, NY, lambda k: greet((2 * ((y + k) % NY) + 1 - core, e)))
    pl.semaphore_wait(barrier, EX - 1 + PEERS - NX + NY)
    others = pl.ds(0, SLOTS - CAP)
    own_rows = pl.ds(pl.multiple_of(e * CAP, CAP), CAP)

    def y_copy(k):
        px, py, device = plane(k)
        return remote(y_send.at[px * NY + py], y_recv.at[me], ys_sem, yr_sem, device)

    repeat(1, PEERS, lambda k: y_copy(k).start())
    drain.append((y_send.at[pl.ds(0, PEERS - 1)], ys_sem))
    y_recv[me] = y_send[me]

    def full_rows(which):
        return full_out.at[pl.ds(pl.multiple_of(which * rows, 128), rows)]

    def full_copy(k):
        py = (y + k) % NY
        return remote(
            own_proj, full_rows(d), fs_sem, fr_sem.at[k], (2 * py + core, e)
        )

    def up_copy(k):
        view = full_rows(2 * ((y + NY - k) % NY) + core)
        return remote(own_proj if k == 0 else view, view, us_sem, ur_sem, sibling)

    own_full = pltpu.make_async_copy(own_proj, full_rows(d), loc_sem)
    own_full.start()
    for k in range(1, NY):
        full_copy(k).start()
    up_copy(0).start()
    own_full.wait()
    drain.append((full_out.at[pl.ds(0, (NY - 1) * rows)], fs_sem))
    drain.append((full_out.at[pl.ds(0, NY * rows)], us_sem))
    drain.append((full_out.at[pl.ds(0, NY * rows)], ur_sem))

    def up_rest():
        for k in range(1, NY):
            full_copy(k).wait_recv()
            up_copy(k).start()

    settle(y_recv.at[pl.ds(0, PEERS - 1)], yr_sem)

    def add_up(i):
        chunk = pl.ds(pl.multiple_of(i * 32, 32), 32)
        total[chunk] = jnp.sum(y_recv[:, chunk, :].astype(jnp.float32), axis=0).astype(
            jnp.bfloat16
        )

    repeat(0, tokens // 32, add_up)

    def sort_total(i):
        chunk = pl.ds(pl.multiple_of(i * 128, 128), 128)
        a_send[chunk] = jnp.dot(
            one_hot(pos_target[0:1], i * 128, 128),
            total[...],
            preferred_element_type=jnp.float32,
        ).astype(jnp.bfloat16)

    repeat(0, SLOTS // 128, sort_total)

    def alg_copy(k):
        to = (e + k) % EX
        return remote(
            a_send.at[pl.ds(pl.multiple_of(to * CAP, CAP), CAP)],
            a_recv.at[pl.ds(pl.multiple_of(e * CAP, CAP), CAP)],
            as_sem,
            ar_sem,
            (d, to),
        )

    repeat(1, EX, lambda k: alg_copy(k).start())
    drain.append((a_send.at[others], as_sem))
    a_recv[own_rows] = a_send[own_rows]
    settle(a_recv.at[others], ar_sem)

    ff = p_send.shape[1]

    def outer(part):
        p_send[part] = lax.dot_general(
            h_recv[:, pl.ds(pl.multiple_of(part * ff, ff), ff)],
            a_recv[...],
            CONTRACT_ROWS,
            preferred_element_type=jnp.float32,
        ).astype(jnp.bfloat16)

    repeat(0, 2 * NY, outer)

    def pg_copy(k):
        to = (d + k) % (2 * NY)
        return remote(p_send.at[to], p_recv.at[d], gs_sem, gr_sem, (to, e))

    repeat(1, 2 * NY, lambda k: pg_copy(k).start())
    drain.append((p_send.at[pl.ds(0, 2 * NY - 1)], gs_sem))
    p_recv[d] = p_send[d]
    up_rest()
    settle(p_recv.at[pl.ds(0, 2 * NY - 1)], gr_sem)

    def finish(i):
        chunk = pl.ds(pl.multiple_of(i * 32, 32), 32)
        pg_out[chunk] = jnp.sum(p_recv[:, chunk, :].astype(jnp.float32), axis=0)

    repeat(0, ff // 32, finish)

    for view, sem in drain:
        settle(view, sem)


def projected(shift_mask, grad, hidden, act4, pos_home, pos_target, old, new):
    tokens, width = grad.shape
    ff = hidden.shape[1]
    rank = act4.shape[2]
    share = rank // (2 * NY)
    bf16, f32 = jnp.bfloat16, jnp.float32
    vmem = pl.BlockSpec(memory_space=pltpu.VMEM)
    hbm = pl.BlockSpec(memory_space=pl.ANY)
    dma = pltpu.SemaphoreType.DMA
    return pl.pallas_call(
        project_kernel,
        out_shape=(
            jax.ShapeDtypeStruct((PEERS, tokens, rank), bf16),
            jax.ShapeDtypeStruct((old.shape[0], rank), bf16),
            jax.ShapeDtypeStruct((SLOTS, ff), bf16),
            jax.ShapeDtypeStruct((rank, rank), f32),
        ),
        in_specs=[pl.BlockSpec(memory_space=pltpu.SMEM), hbm] + [vmem] * 6,
        out_specs=(vmem,) * 4,
        scratch_shapes=[
            pltpu.VMEM((PEERS, tokens, 512), bf16),
            pltpu.VMEM((PEERS, 8, tokens), jnp.int32),
            pltpu.VMEM((NX, NZ, 512, rank), bf16),
            pltpu.VMEM((EX, PEERS * CAP, 512), bf16),
            pltpu.VMEM((EX, PEERS * CAP, rank), bf16),
            pltpu.VMEM((SLOTS, ff), bf16),
            pltpu.VMEM((NX, 256, rank), bf16),
            pltpu.VMEM((2 * NY, share, rank), f32),
            pltpu.VMEM((2 * NY, share, rank), f32),
            pltpu.VMEM((share, rank), f32),
            dma((4,)),
            dma,
            dma,
            dma,
            dma((PEERS,)),
            dma,
            dma((PEERS,)),
            dma((HALF,)),
            dma((HALF,)),
            dma((HALF,)),
            dma((HALF,)),
            dma((NZ,)),
            dma((NZ,)),
            dma,
            dma,
            dma,
            dma,
            dma,
            dma,
            dma,
            dma,
        ],
        compiler_params=pltpu.CompilerParams(
            collective_id=0, has_side_effects=True, vmem_limit_bytes=60 * 1024 * 1024
        ),
        name="project_tokens",
    )(shift_mask, grad, hidden, act4, pos_home, pos_target, old, new)


def combined(y_parts, own_proj, hidden_rows, pos_target):
    peers, tokens, rank = y_parts.shape
    ff = hidden_rows.shape[1]
    group = 2 * NY
    bf16 = jnp.bfloat16
    vmem = pl.BlockSpec(memory_space=pltpu.VMEM)
    hbm = pl.BlockSpec(memory_space=pl.ANY)
    dma = pltpu.SemaphoreType.DMA
    return pl.pallas_call(
        combine_kernel,
        out_shape=(
            jax.ShapeDtypeStruct((ff // group, rank), jnp.float32),
            jax.ShapeDtypeStruct((WIDTH, rank), bf16),
        ),
        in_specs=[vmem] * 4,
        out_specs=(vmem, hbm),
        scratch_shapes=[
            pltpu.VMEM((PEERS, tokens, rank), bf16),
            pltpu.VMEM((SLOTS, rank), bf16),
            pltpu.VMEM((SLOTS, rank), bf16),
            pltpu.VMEM((group, ff // group, rank), bf16),
            pltpu.VMEM((group, ff // group, rank), bf16),
            pltpu.VMEM((tokens, rank), bf16),
            dma,
            dma,
            dma,
            dma,
            dma,
            dma,
            dma,
            dma,
            dma((NY,)),
            dma,
            dma,
        ],
        compiler_params=pltpu.CompilerParams(
            collective_id=1, has_side_effects=True, vmem_limit_bytes=48 * 1024 * 1024
        ),
        cost_estimate=pl.CostEstimate(
            flops=1_000_000_000, bytes_accessed=300_000_000, transcendentals=0
        ),
        name="combine_rows",
    )(y_parts, own_proj, hidden_rows, pos_target)


def moved(packed, operands, shift_mask):
    experts = lax.axis_size("expert")

    def leaf(mask):
        pairs = [(source, source ^ mask) for source in range(experts)]

        def branch(array, inputs):
            return (lax.ppermute(array, "expert", pairs),) + tuple(combined(*inputs))

        return branch

    def tree(low, high):
        if high - low == 1:
            return leaf(low)
        middle = (low + high) // 2
        below, above = tree(low, middle), tree(middle, high)
        return lambda array, inputs: lax.cond(
            shift_mask < middle, below, above, array, inputs
        )

    return tree(1, experts)(packed, operands)


def per_device(
    weight,
    first_moment,
    second_moment,
    projector_old,
    projector_new,
    change_flag,
    partner,
    hidden_act,
    out_grad,
    route,
):
    own_index = lax.axis_index("expert")
    shift_mask = partner[0]
    changed = change_flag[own_index] > 0
    old_proj, new_proj = projector_old[0], projector_new[0]
    active_home = jnp.where(changed, new_proj, old_proj)
    home = route[:, 0]
    columns = jnp.arange(EX, dtype=jnp.int32)
    picked = (home[:, None] == columns[None, :]).astype(jnp.int32)
    rank_of = jnp.sum((jnp.cumsum(picked, axis=0) - picked) * picked, axis=1)
    tokens = home.shape[0]
    pos_home = jnp.broadcast_to((home * CAP + rank_of)[None, :], (8, tokens))
    pos_target = jnp.broadcast_to(
        (jnp.bitwise_xor(home, shift_mask) * CAP + rank_of)[None, :], (8, tokens)
    )
    act4 = jnp.stack(
        [
            active_home[0:256],
            active_home[256:512],
            active_home[512:768],
            jnp.concatenate([jnp.zeros_like(active_home[:128]), active_home[768:896]], axis=0),
        ]
    )
    y_parts, active, hidden_rows, intersection = projected(
        partner[:1], out_grad, hidden_act, act4, pos_home, pos_target, old_proj, new_proj
    )
    first_turned = jnp.dot(first_moment[0], intersection, precision=lax.Precision.HIGHEST)
    second_turned = jnp.dot(
        second_moment[0], intersection * intersection, precision=lax.Precision.HIGHEST
    )
    first_start = jnp.where(changed, first_turned, first_moment[0]).astype(jnp.bfloat16)
    second_start = jnp.where(changed, second_turned, second_moment[0]).astype(jnp.bfloat16)
    packed, proj_grad, projector_full = moved(
        jnp.concatenate([weight[0], first_start, second_start], axis=1),
        (y_parts, active, hidden_rows, pos_target),
        shift_mask,
    )
    width, rank = weight.shape[2], first_start.shape[1]
    weight_here = packed[:, :width]
    first_start = packed[:, width : width + rank]
    second_start = packed[:, width + rank :]
    first_next = beta_one * first_start.astype(jnp.float32) + (1.0 - beta_one) * proj_grad
    second_next = (
        beta_two * second_start.astype(jnp.float32) + (1.0 - beta_two) * proj_grad * proj_grad
    )
    direction = (first_next / (jnp.sqrt(second_next) + adam_eps)).astype(jnp.bfloat16)
    update = lax.dot_general(
        direction, projector_full, (((1,), (1,)), ((), ())), preferred_element_type=jnp.float32
    )
    new_weight = (weight_here.astype(jnp.float32) - step_size * update).astype(jnp.bfloat16)
    return (new_weight[None], first_next[None], second_next[None], active[None])


def solution(mesh):
    in_specs = (
        P("expert", "dp", None),
        P("expert", "dp", None),
        P("expert", "dp", None),
        P("expert", "dp", None),
        P("expert", "dp", None),
        P(),
        P(),
        P(("dp", "expert"), None),
        P(("dp", "expert"), None),
        P(("dp", "expert"), None),
    )
    out_specs = (
        P("expert", "dp", None),
        P("expert", "dp", None),
        P("expert", "dp", None),
        P("expert", "dp", None),
    )
    return jax.shard_map(
        per_device, mesh=mesh, in_specs=in_specs, out_specs=out_specs, check_vma=False
    )
```
